32 devices in a mesh: group: 2 (over x), tp: 8 (over z, y), dp: 2 (over core).
Axes of the slice: x: 2, y: 2, z: 4, core: 2. Of those that a mesh axis runs over, the one named last changes fastest.
Arguments:
- gate_up: bfloat16 [4096, 2, 14336], P(('group', 'dp'), None, 'tp'), parts along dimension 0, may hold values from -6 to 6
- residual: bfloat16 [4096, 8192], P(('group', 'dp'), 'tp'), parts along dimension 0, may hold values from -40 to 40
- down_weight: bfloat16 [14336, 8192], P('tp'), may hold values from -0.046875 to 0.046875
- shrink_weight: bfloat16 [16, 14336, 64], P(None, 'tp'), may hold values from -0.046875 to 0.046875
- expand_weight: bfloat16 [16, 64, 8192], P(None, None, 'tp'), may hold values from -0.75 to 0.75
- block_adapter: int32 [128], P(('group', 'dp')), parts along dimension 0, may hold values from 0 to 15
- adapter_slot: int32 [16], replicated, may hold values from 0 to 15, each once
- norm_gain: bfloat16 [8192], P('tp'), may hold values from 0.099609375 to 1.8984375
Outputs:
- updated: bfloat16 [4096, 8192], P(('group', 'dp'), 'tp'), parts along dimension 0
- normed: bfloat16 [4096, 8192], P(('group', 'dp'), 'tp'), parts along dimension 0
The draws below stay inside these ranges and needn't reach their ends.
There are 2 independent parts, one for each index of `group`. The reference program is written for one: setup_inputs(seed, part) draws one part's arguments, and reference() takes and returns one part's arrays. A program takes and returns all parts, laid end to end along the dimension named above; an argument that names none is the same for every part. Nothing has to cross between parts.
All inputs are finite; a program needn't handle non-finite values.
Results may differ from the reference program's by a relative error of at most 0.009.
Values may be sent and summed in bfloat16 or wider, within the bound.
A program may use at most 192 MiB of HBM per device.

```python
import math
import jax
import jax.numpy as jnp
import numpy as np
from jax import lax

MODEL_WIDTH = 8192
FF = 14336
R = 64
ADAPT = 16
BLOCK = 32
DECODE_ROWS = 2048
NBLK = 64
N_TP = 8


def draw_residual(key, part):
    key = jax.random.fold_in(key, 11)
    key_rows, key_cols, key_main = jax.random.split(key, 3)
    row_scale = jnp.exp(jax.random.uniform(key_rows, (DECODE_ROWS, 1), jnp.float32, math.log(0.3), math.log(3.0)))
    ramp = 0.6 * jnp.power(3.0, jnp.arange(MODEL_WIDTH, dtype=jnp.float32) / MODEL_WIDTH)[None, :]
    col_scale = ramp * jnp.exp(jax.random.uniform(key_cols, (1, MODEL_WIDTH), jnp.float32, math.log(0.7), math.log(1.4)))
    values = jnp.clip(jax.random.normal(key_main, (DECODE_ROWS, MODEL_WIDTH), jnp.float32), -5.0, 5.0)
    return (row_scale * col_scale * values).astype(jnp.bfloat16)


def touch_ends(result, own_key, smallest, top_value):
    index_at = [jax.random.randint(jax.random.fold_in(own_key, axis), (), 0, length) for axis, length in enumerate(result.shape)]
    main_axis = result.shape.index(max(result.shape))
    neighbour = index_at[:main_axis] + [(index_at[main_axis] + 1) % result.shape[main_axis]] + index_at[main_axis + 1:]
    return result.at[tuple(index_at)].set(smallest).at[tuple(neighbour)].set(top_value)


def block_levels(rng, extent, pieces, least, largest):
    gain, own = 1.0, jax.random.fold_in(rng, 6)
    for dim, shards_of in pieces:
        draws = jnp.exp(jax.random.uniform(jax.random.fold_in(own, dim), (shards_of,), jnp.float32, least / len(pieces), largest / len(pieces)))
        gain = gain * jnp.repeat(draws, extent[dim] // shards_of).reshape([-1 if axis == dim else 1 for axis in range(len(extent))])
    return gain


def cumulative_ranks(count, lean):
    portions = [(1 << 20) // math.isqrt(grade ** lean) + 1 for grade in range(1, count + 1)]
    deviation = 1 + sum(portions) // (1 << 30)
    return np.cumsum(np.array([max(1, weight // deviation) for weight in portions]))


def ranked(key, dims, amount, skew):
    listing = cumulative_ranks(amount, skew)
    lot = jax.random.randint(jax.random.fold_in(key, 1), dims, 0, int(listing[amount - 1]))
    standing = jnp.searchsorted(jnp.asarray(listing, jnp.int32), lot, side="right")
    return jax.random.permutation(jax.random.fold_in(key, 2), amount)[standing].astype(jnp.int32)


def normal_values(key, extent, spread, limit, cuts=(), kind=jnp.bfloat16):
    array = jax.random.normal(key, extent, jnp.float32) * spread
    if len(cuts) > 0:
        array = block_levels(key, extent, cuts, -0.22, 0.18) * array
    return jnp.clip(array, min=-limit, max=limit).astype(kind)


def setup_inputs(seed: int = 0, part: int = 0) -> dict:
    keys = jax.random.split(jax.random.key(seed), 9)
    own_keys = jax.random.split(jax.random.fold_in(keys[8], part), 9)
    return {
        "gate_up": normal_values(own_keys[0], (DECODE_ROWS, 2, FF), 1.0, 6.0, ((0, 2), (2, 8))),
        "residual": draw_residual(jax.random.fold_in(jax.random.fold_in(keys[8], part), 71), part),
        "down_weight": normal_values(keys[2], (FF, MODEL_WIDTH), FF ** -0.5, 0.046875, ((0, 8),)),
        "shrink_weight": normal_values(keys[3], (ADAPT, FF, R), FF ** -0.5, 0.046875, ((1, 8),)),
        "expand_weight": normal_values(keys[4], (ADAPT, R, MODEL_WIDTH), R ** -0.5, 0.75, ((2, 8),)),
        "block_adapter": touch_ends(ranked(own_keys[5], (NBLK,), ADAPT, 2), jax.random.fold_in(own_keys[5], 3), 0, ADAPT - 1).astype(jnp.int32),
        "adapter_slot": jax.random.permutation(keys[6], ADAPT).astype(jnp.int32),
        "norm_gain": jnp.clip(1.0 + 0.18 * jax.random.normal(keys[7], (MODEL_WIDTH,), jnp.float32), 0.099609375, 1.8984375).astype(jnp.bfloat16),
    }


adapter_scale = 0.5

def reference(gate_up, residual, down_weight, shrink_weight, expand_weight, block_adapter, adapter_slot, norm_gain):
    gate_val = gate_up[:, 0, :].astype(jnp.float32)
    up_val = gate_up[:, 1, :].astype(jnp.float32)
    hidden = (jax.nn.silu(gate_val) * up_val).astype(jnp.bfloat16)
    part_cols = FF // N_TP

    def add_part(index, accum):
        hidden_part = lax.dynamic_slice_in_dim(hidden, index * part_cols, part_cols, 1)
        weight_part = lax.dynamic_slice_in_dim(down_weight, index * part_cols, part_cols, 0)
        term = jnp.dot(hidden_part, weight_part, preferred_element_type=jnp.float32)
        rounded = lax.optimization_barrier(term.astype(jnp.bfloat16)).astype(jnp.float32)
        return accum + rounded
    projection_sum = lax.fori_loop(0, N_TP, add_part, jnp.zeros((DECODE_ROWS, MODEL_WIDTH), jnp.float32))
    slot_ids = adapter_slot[block_adapter].astype(jnp.int32)
    stacked = hidden.reshape(NBLK, BLOCK, FF).astype(jnp.float32)
    picked = shrink_weight[slot_ids].astype(jnp.float32)
    shrunk_rows = jnp.einsum('bkf,bfr->bkr', stacked, picked).astype(jnp.bfloat16)
    expand_selected = expand_weight[slot_ids].astype(jnp.float32)
    adapter_term = jnp.einsum('xcf,xfe->xce', shrunk_rows.astype(jnp.float32), expand_selected).reshape(DECODE_ROWS, MODEL_WIDTH)
    updated = (residual.astype(jnp.float32) + projection_sum + adapter_scale * adapter_term).astype(jnp.bfloat16)
    widened = updated.astype(jnp.float32)
    mean_sq = lax.optimization_barrier(jnp.mean(widened * widened, axis=1, keepdims=True))
    normed = (widened * lax.rsqrt(mean_sq + 1e-05) * norm_gain.astype(jnp.float32)[None, :]).astype(jnp.bfloat16)
    return (updated, normed)
```

```python
import functools

import jax
import jax.numpy as jnp
from jax import lax
from jax.experimental import pallas as pl
from jax.experimental.pallas import tpu as pltpu
from jax.sharding import PartitionSpec as P

MODEL_WIDTH = 8192
CHUNK_ROWS = 128
COL_TILE = 256


adapter_scale = 0.5


def project_kernel(depth, pair, chunks, h_ref, w_hbm, out_ref, w_vmem, outgoing, held, landed, acc,
                   w_sem, pair_send, pair_recv, line_send, line_recv):
    me = lax.axis_index("tp")
    pos = me // pair
    side = me % pair
    rows = CHUNK_ROWS
    width = acc.shape[1]
    tile = min(COL_TILE, width)
    toward = 2 * (pos // (depth // 2)) - 1

    def target(j):
        return (pos + toward * (1 + j) + depth) % depth

    def w_copy(block):
        return pltpu.make_async_copy(
            w_hbm.at[:, pl.ds(pl.multiple_of(block * width, width), width)],
            w_vmem.at[block], w_sem.at[block])

    def pair_copy(chunk, dest):
        return pltpu.make_async_remote_copy(
            src_ref=outgoing.at[chunk % 2, dest], dst_ref=held.at[chunk, dest],
            send_sem=pair_send.at[chunk, dest], recv_sem=pair_recv.at[chunk, dest],
            device_id={"tp": pos * pair + (1 - side)}, device_id_type=pl.DeviceIdType.MESH)

    def line_copy(chunk, dest, slot, to):
        return pltpu.make_async_remote_copy(
            src_ref=held.at[chunk, dest], dst_ref=landed.at[chunk, slot],
            send_sem=line_send.at[chunk, dest], recv_sem=line_recv.at[chunk, slot],
            device_id={"tp": to * pair + side}, device_id_type=pl.DeviceIdType.MESH)

    barrier = pltpu.get_barrier_semaphore()
    if pair > 1:
        pl.semaphore_signal(barrier, inc=1, device_id={"tp": pos * pair + (1 - side)},
                            device_id_type=pl.DeviceIdType.MESH)

    @pl.when(pos > 0)
    def _():
        pl.semaphore_signal(barrier, inc=1, device_id={"tp": me - pair},
                            device_id_type=pl.DeviceIdType.MESH)

    @pl.when(pos < depth - 1)
    def _():
        pl.semaphore_signal(barrier, inc=1, device_id={"tp": me + pair},
                            device_id_type=pl.DeviceIdType.MESH)

    def start_w(j, _):
        if pair > 1:
            w_copy(target(j) * pair + (1 - side)).start()
        return 0

    lax.fori_loop(0, depth, start_w, 0)

    def start_w_own(j, _):
        w_copy(target(j) * pair + side).start()
        return 0

    lax.fori_loop(0, depth, start_w_own, 0)

    pl.semaphore_wait(
        barrier, pair - 1 + jnp.minimum(pos, 1) + jnp.minimum(depth - 1 - pos, 1))

    def lines(chunk):
        return pl.ds(pl.multiple_of(chunk * rows, rows), rows)

    def offer(chunk):
        def one(j, _):
            dest = target(j)
            block = dest * pair + (1 - side)

            @pl.when(chunk == 0)
            def _():
                w_copy(block).wait()

            @pl.when(chunk >= 2)
            def _():
                pair_copy(chunk - 2, dest).wait_send()

            def col(n, _):
                cols = pl.ds(pl.multiple_of(n * tile, tile), tile)
                outgoing[chunk % 2, dest, :, cols] = jnp.dot(
                    h_ref[lines(chunk), :], w_vmem[block, :, cols],
                    preferred_element_type=jnp.float32).astype(jnp.bfloat16)
                return 0

            lax.fori_loop(0, width // tile, col, 0)
            pair_copy(chunk, dest).start()
            return 0

        lax.fori_loop(0, depth, one, 0)

    def gather_own(chunk, dest):
        block = dest * pair + side

        @pl.when(chunk == 0)
        def _():
            w_copy(block).wait()

        def col(n, _):
            cols = pl.ds(pl.multiple_of(n * tile, tile), tile)
            acc[:, cols] = jnp.dot(h_ref[lines(chunk), :], w_vmem[block, :, cols],
                                   preferred_element_type=jnp.float32)
            return 0

        lax.fori_loop(0, width // tile, col, 0)
        if pair > 1:
            pair_copy(chunk, dest).wait_recv()
            acc[...] += held[chunk, dest].astype(jnp.float32)

    def take(chunk, slot):
        line_copy(chunk, 0, slot, pos).wait_recv()
        acc[...] += landed[chunk, slot].astype(jnp.float32)

    def forward(chunk, dest, up):
        gather_own(chunk, dest)
        if up:
            @pl.when(pos > 0)
            def _():
                take(chunk, dest)
            held[chunk, dest] = acc[...].astype(jnp.bfloat16)
            line_copy(chunk, dest, dest, pos + 1).start()
        else:
            @pl.when(pos < depth - 1)
            def _():
                take(chunk, dest)
            held[chunk, dest] = acc[...].astype(jnp.bfloat16)
            slot = dest + (depth - dest) * (1 - jnp.minimum(pos - 1 - dest, 1))
            line_copy(chunk, dest, slot, pos - 1).start()

    def send_up(chunk):
        def one(j, _):
            forward(chunk, depth - 1 - j, True)
            return 0

        lax.fori_loop(0, depth - 1 - pos, one, 0)

    def send_down(chunk):
        def one(j, _):
            forward(chunk, j, False)
            return 0

        lax.fori_loop(0, pos, one, 0)

    def keep(chunk):
        gather_own(chunk, pos)

        @pl.when(pos > 0)
        def _():
            take(chunk, pos)

        @pl.when(pos < depth - 1)
        def _():
            take(chunk, depth)

        out_ref[lines(chunk), :] = acc[...]

    def step(k, _):
        if pair > 1:
            @pl.when(k < chunks)
            def _():
                offer(k)

        upward = k - 1 - pos
        downward = k - depth + pos

        @pl.when(jnp.logical_and(upward >= 0, upward < chunks))
        def _():
            send_up(upward)

        @pl.when(jnp.logical_and(downward >= 0, downward < chunks))
        def _():
            send_down(downward)

        last = jnp.minimum(upward, downward)

        @pl.when(jnp.logical_and(last >= 0, last < chunks))
        def _():
            keep(last)
        return 0

    lax.fori_loop(0, chunks + depth, step, 0)

    def finish(chunk, _):
        def one(dest, _):
            @pl.when(dest != pos)
            def _():
                line_copy(chunk, dest, dest, pos).wait_send()
            if pair > 1:
                @pl.when(chunk >= chunks - 2)
                def _():
                    pair_copy(chunk, dest).wait_send()
            return 0

        lax.fori_loop(0, depth, one, 0)
        return 0

    lax.fori_loop(0, chunks, finish, 0)


def project(hidden, down_weight, depth, pair):
    count, inner = hidden.shape
    width = down_weight.shape[1] // (depth * pair)
    chunks = count // CHUNK_ROWS
    block = (CHUNK_ROWS, width)
    return pl.pallas_call(
        functools.partial(project_kernel, depth, pair, chunks),
        out_shape=jax.ShapeDtypeStruct((count, width), jnp.float32),
        in_specs=[pl.BlockSpec(memory_space=pltpu.VMEM), pl.BlockSpec(memory_space=pl.ANY)],
        out_specs=pl.BlockSpec(memory_space=pltpu.VMEM),
        scratch_shapes=[
            pltpu.VMEM((depth * pair, inner, width), jnp.bfloat16),
            pltpu.VMEM((2, depth if pair > 1 else 1) + block, jnp.bfloat16),
            pltpu.VMEM((chunks, depth) + block, jnp.bfloat16),
            pltpu.VMEM((chunks, depth + 1) + block, jnp.bfloat16),
            pltpu.VMEM(block, jnp.float32),
            pltpu.SemaphoreType.DMA((depth * pair,)),
            pltpu.SemaphoreType.DMA((chunks, depth)),
            pltpu.SemaphoreType.DMA((chunks, depth)),
            pltpu.SemaphoreType.DMA((chunks, depth)),
            pltpu.SemaphoreType.DMA((chunks, depth + 1)),
        ],
        compiler_params=pltpu.CompilerParams(
            collective_id=0, has_side_effects=True, vmem_limit_bytes=60 * 1024 * 1024),
        cost_estimate=pl.CostEstimate(
            flops=2 * count * inner * down_weight.shape[1],
            bytes_accessed=200_000_000, transcendentals=0),
    )(hidden, down_weight)


def on_device(
    depth,
    pair,
    gate_up,
    residual,
    down_weight,
    shrink_weight,
    expand_weight,
    block_adapter,
    adapter_slot,
    norm_gain,
):
    gate_val = gate_up[:, 0, :].astype(jnp.float32)
    up_val = gate_up[:, 1, :].astype(jnp.float32)
    hidden = (jax.nn.silu(gate_val) * up_val).astype(jnp.bfloat16)
    count_of_rows, ff_local = hidden.shape
    blocks = block_adapter.shape[0]
    block_rows = count_of_rows // blocks
    adapters = adapter_slot.shape[0]
    rank = shrink_weight.shape[2]
    column_count = expand_weight.shape[2]
    adapter_range = jnp.arange(adapters, dtype=jnp.int32)
    chosen = block_adapter[:, None] == adapter_range[None, :]
    slot_ids = jnp.sum(jnp.where(chosen, adapter_slot[None, :], 0), axis=1)
    stacked = hidden.reshape(blocks, block_rows, ff_local)
    picked = shrink_weight[slot_ids]
    rank_terms = jnp.einsum("bkf,bfr->bkr", stacked, picked, preferred_element_type=jnp.float32)
    shrunk_rows = lax.psum(rank_terms.astype(jnp.bfloat16), "tp")
    projection_sum = project(hidden, down_weight, depth, pair)
    at_slot = (slot_ids[:, None] == adapter_range[None, :]).astype(jnp.bfloat16)
    spread = (shrunk_rows[:, :, None, :] * at_slot[:, None, :, None]).reshape(
        count_of_rows, adapters * rank)
    adapter_term = jnp.dot(
        spread, expand_weight.reshape(adapters * rank, column_count),
        preferred_element_type=jnp.float32)
    updated = (residual.astype(jnp.float32) + projection_sum + adapter_scale * adapter_term).astype(
        jnp.bfloat16
    )
    widened = updated.astype(jnp.float32)
    square_tot = lax.psum(jnp.sum(widened * widened, axis=1), "tp")
    mean_sq = square_tot[:, None] / MODEL_WIDTH
    normed = (widened * lax.rsqrt(mean_sq + 1e-05) * norm_gain.astype(jnp.float32)[None, :]).astype(
        jnp.bfloat16
    )
    return (updated, normed)


def solution(mesh):
    in_specs = (
        P(("group", "dp"), None, "tp"),
        P(("group", "dp"), "tp"),
        P("tp", None),
        P(None, "tp", None),
        P(None, None, "tp"),
        P(("group", "dp")),
        P(),
        P("tp"),
    )
    out_specs = (P(("group", "dp"), "tp"), P(("group", "dp"), "tp"))
    pair = max(1, 4 // mesh.shape["group"])
    depth = mesh.shape["tp"] // pair
    return jax.shard_map(
        functools.partial(on_device, depth, pair),
        mesh=mesh, in_specs=in_specs, out_specs=out_specs, check_vma=False
    )
```

```python
import functools

import jax
import jax.numpy as jnp
from jax import lax
from jax.experimental import pallas as pl
from jax.experimental.pallas import tpu as pltpu
from jax.sharding import PartitionSpec as P

MODEL_WIDTH = 8192
CHUNK_ROWS = 128
COL_TILE = 256


adapter_scale = 0.5


def project_kernel(depth, pair, chunks, h_ref, w_hbm, out_ref, w_vmem, outgoing, held, landed, acc,
                   w_sem, pair_send, pair_recv, line_send, line_recv):
    me = lax.axis_index("tp")
    pos = me // pair
    side = me % pair
    rows = CHUNK_ROWS
    width = acc.shape[1]
    tile = min(COL_TILE, width)
    toward = 2 * (pos // (depth // 2)) - 1

    def target(j):
        return (pos + toward * (1 + j) + depth) % depth

    def w_copy(block):
        return pltpu.make_async_copy(
            w_hbm.at[:, pl.ds(pl.multiple_of(block * width, width), width)],
            w_vmem.at[block], w_sem.at[block])

    def pair_copy(chunk, dest):
        return pltpu.make_async_remote_copy(
            src_ref=outgoing.at[chunk % 2, dest], dst_ref=held.at[chunk, dest],
            send_sem=pair_send.at[chunk, dest], recv_sem=pair_recv.at[chunk, dest],
            device_id={"tp": pos * pair + (1 - side)}, device_id_type=pl.DeviceIdType.MESH)

    def line_copy(chunk, dest, slot, to):
        return pltpu.make_async_remote_copy(
            src_ref=held.at[chunk, dest], dst_ref=landed.at[chunk, slot],
            send_sem=line_send.at[chunk, dest], recv_sem=line_recv.at[chunk, slot],
            device_id={"tp": to * pair + side}, device_id_type=pl.DeviceIdType.MESH)

    barrier = pltpu.get_barrier_semaphore()
    if pair > 1:
        pl.semaphore_signal(barrier, inc=1, device_id={"tp": pos * pair + (1 - side)},
                            device_id_type=pl.DeviceIdType.MESH)

    @pl.when(pos > 0)
    def _():
        pl.semaphore_signal(barrier, inc=1, device_id={"tp": me - pair},
                            device_id_type=pl.DeviceIdType.MESH)

    @pl.when(pos < depth - 1)
    def _():
        pl.semaphore_signal(barrier, inc=1, device_id={"tp": me + pair},
                            device_id_type=pl.DeviceIdType.MESH)

    def start_w(j, _):
        if pair > 1:
            w_copy(target(j) * pair + (1 - side)).start()
        return 0

    lax.fori_loop(0, depth, start_w, 0)

    def start_w_own(j, _):
        w_copy(target(j) * pair + side).start()
        return 0

    lax.fori_loop(0, depth, start_w_own, 0)

    pl.semaphore_wait(
        barrier, pair - 1 + jnp.minimum(pos, 1) + jnp.minimum(depth - 1 - pos, 1))

    def lines(chunk):
        return pl.ds(pl.multiple_of(chunk * rows, rows), rows)

    def offer(chunk):
        def one(j, _):
            dest = target(j)
            block = dest * pair + (1 - side)

            @pl.when(chunk == 0)
            def _():
                w_copy(block).wait()

            @pl.when(chunk >= 2)
            def _():
                pair_copy(chunk - 2, dest).wait_send()

            def col(n, _):
                cols = pl.ds(pl.multiple_of(n * tile, tile), tile)
                outgoing[chunk % 2, dest, :, cols] = jnp.dot(
                    h_ref[lines(chunk), :], w_vmem[block, :, cols],
                    preferred_element_type=jnp.float32).astype(jnp.bfloat16)
                return 0

            lax.fori_loop(0, width // tile, col, 0)
            pair_copy(chunk, dest).start()
            return 0

        lax.fori_loop(0, depth, one, 0)

    def gather_own(chunk, dest):
        block = dest * pair + side

        @pl.when(chunk == 0)
        def _():
            w_copy(block).wait()

        def col(n, _):
            cols = pl.ds(pl.multiple_of(n * tile, tile), tile)
            acc[:, cols] = jnp.dot(h_ref[lines(chunk), :], w_vmem[block, :, cols],
                                   preferred_element_type=jnp.float32)
            return 0

        lax.fori_loop(0, width // tile, col, 0)
        if pair > 1:
            pair_copy(chunk, dest).wait_recv()
            acc[...] += held[chunk, dest].astype(jnp.float32)

    def take(chunk, slot):
        line_copy(chunk, 0, slot, pos).wait_recv()
        acc[...] += landed[chunk, slot].astype(jnp.float32)

    def forward(chunk, dest, up):
        gather_own(chunk, dest)
        if up:
            @pl.when(pos > 0)
            def _():
                take(chunk, dest)
            held[chunk, dest] = acc[...].astype(jnp.bfloat16)
            line_copy(chunk, dest, dest, pos + 1).start()
        else:
            @pl.when(pos < depth - 1)
            def _():
                take(chunk, dest)
            held[chunk, dest] = acc[...].astype(jnp.bfloat16)
            slot = dest + (depth - dest) * (1 - jnp.minimum(pos - 1 - dest, 1))
            line_copy(chunk, dest, slot, pos - 1).start()

    def send_up(chunk):
        def one(j, _):
            forward(chunk, depth - 1 - j, True)
            return 0

        lax.fori_loop(0, depth - 1 - pos, one, 0)

    def send_down(chunk):
        def one(j, _):
            forward(chunk, j, False)
            return 0

        lax.fori_loop(0, pos, one, 0)

    def keep(chunk):
        gather_own(chunk, pos)

        @pl.when(pos > 0)
        def _():
            take(chunk, pos)

        @pl.when(pos < depth - 1)
        def _():
            take(chunk, depth)

        out_ref[lines(chunk), :] = acc[...]

    def step(k, _):
        if pair > 1:
            @pl.when(k < chunks)
            def _():
                offer(k)

        upward = k - 1 - pos
        downward = k - depth + pos

        @pl.when(jnp.logical_and(upward >= 0, upward < chunks))
        def _():
            send_up(upward)

        @pl.when(jnp.logical_and(downward >= 0, downward < chunks))
        def _():
            send_down(downward)

        last = jnp.minimum(upward, downward)

        @pl.when(jnp.logical_and(last >= 0, last < chunks))
        def _():
            keep(last)
        return 0

    lax.fori_loop(0, chunks + depth, step, 0)

    def finish(chunk, _):
        def one(dest, _):
            @pl.when(dest != pos)
            def _():
                line_copy(chunk, dest, dest, pos).wait_send()
            if pair > 1:
                @pl.when(chunk >= chunks - 2)
                def _():
                    pair_copy(chunk, dest).wait_send()
            return 0

        lax.fori_loop(0, depth, one, 0)
        return 0

    lax.fori_loop(0, chunks, finish, 0)


def project(hidden, down_weight, depth, pair):
    count, inner = hidden.shape
    width = down_weight.shape[1] // (depth * pair)
    chunks = count // CHUNK_ROWS
    block = (CHUNK_ROWS, width)
    return pl.pallas_call(
        functools.partial(project_kernel, depth, pair, chunks),
        out_shape=jax.ShapeDtypeStruct((count, width), jnp.float32),
        in_specs=[pl.BlockSpec(memory_space=pltpu.VMEM), pl.BlockSpec(memory_space=pl.ANY)],
        out_specs=pl.BlockSpec(memory_space=pltpu.VMEM),
        scratch_shapes=[
            pltpu.VMEM((depth * pair, inner, width), jnp.bfloat16),
            pltpu.VMEM((2, depth if pair > 1 else 1) + block, jnp.bfloat16),
            pltpu.VMEM((chunks, depth) + block, jnp.bfloat16),
            pltpu.VMEM((chunks, depth + 1) + block, jnp.bfloat16),
            pltpu.VMEM(block, jnp.float32),
            pltpu.SemaphoreType.DMA((depth * pair,)),
            pltpu.SemaphoreType.DMA((chunks, depth)),
            pltpu.SemaphoreType.DMA((chunks, depth)),
            pltpu.SemaphoreType.DMA((chunks, depth)),
            pltpu.SemaphoreType.DMA((chunks, depth + 1)),
        ],
        compiler_params=pltpu.CompilerParams(
            collective_id=0, has_side_effects=True, vmem_limit_bytes=60 * 1024 * 1024),
        cost_estimate=pl.CostEstimate(
            flops=2 * count * inner * down_weight.shape[1],
            bytes_accessed=200_000_000, transcendentals=0),
    )(hidden, down_weight)


def slot_mask(slot_rows, group, rank):
    per = 128 // rank
    lane = lax.broadcasted_iota(jnp.int32, slot_rows.shape, 1) // rank
    return slot_rows == group * per + lane


def hidden_kernel(rank, gate_up_ref, shrink_ref, slot_ref, hidden_ref, rank_ref):
    gate = gate_up_ref[:, 0, :].astype(jnp.float32)
    up = gate_up_ref[:, 1, :].astype(jnp.float32)
    hidden = (jax.nn.silu(gate) * up).astype(jnp.bfloat16)
    hidden_ref[...] = hidden
    slot_rows = slot_ref[...]
    total = jnp.zeros(slot_rows.shape, jnp.float32)
    terms = lax.dot_general(hidden, shrink_ref[...], (((1,), (1,)), ((), ())),
                            preferred_element_type=jnp.float32)
    for group in range(shrink_ref.shape[0] // 128):
        part = terms[:, group * 128:(group + 1) * 128]
        total += jnp.where(slot_mask(slot_rows, group, rank), part, 0.0)
    rank_ref[...] = total.astype(jnp.bfloat16)


def hidden_and_rank(gate_up, shrink_flat, slot_rows, rank):
    count, _, inner = gate_up.shape
    rows = 128
    return pl.pallas_call(
        functools.partial(hidden_kernel, rank),
        grid=(count // rows,),
        out_shape=(jax.ShapeDtypeStruct((count, inner), jnp.bfloat16),
                   jax.ShapeDtypeStruct((count, 128), jnp.bfloat16)),
        in_specs=[pl.BlockSpec((rows, 2, inner), lambda i: (i, 0, 0)),
                  pl.BlockSpec(shrink_flat.shape, lambda i: (0, 0)),
                  pl.BlockSpec((rows, 128), lambda i: (i, 0))],
        out_specs=(pl.BlockSpec((rows, inner), lambda i: (i, 0)),
                   pl.BlockSpec((rows, 128), lambda i: (i, 0))),
        compiler_params=pltpu.CompilerParams(vmem_limit_bytes=48 * 1024 * 1024),
    )(gate_up, shrink_flat, slot_rows)


def norm_kernel(size, rank, proj_ref, residual_ref, rank_ref, slot_ref, expand_ref, gain_ref,
                updated_ref, normed_ref, mine, others, send_sem, recv_sem):
    me = lax.axis_index("tp")
    barrier = pltpu.get_barrier_semaphore()

    def greet(j, _):
        pl.semaphore_signal(barrier, inc=1, device_id={"tp": (me + j) % size},
                            device_id_type=pl.DeviceIdType.MESH)
        return 0

    lax.fori_loop(1, size, greet, 0)
    groups = expand_ref.shape[0] // 128
    width = updated_ref.shape[1]
    blocks = mine.shape[0]
    for b in range(blocks):
        rows = slice(b * 128, (b + 1) * 128)
        slot_rows = slot_ref[rows, :]
        values = rank_ref[rows, :].astype(jnp.float32)
        spread = jnp.concatenate(
            [jnp.where(slot_mask(slot_rows, group, rank), values, 0.0) for group in range(groups)],
            axis=1).astype(jnp.bfloat16)
        adapter_term = jnp.dot(spread, expand_ref[...], preferred_element_type=jnp.float32)
        updated = (residual_ref[rows, :].astype(jnp.float32) + proj_ref[rows, :]
                   + adapter_scale * adapter_term).astype(jnp.bfloat16)
        updated_ref[rows, :] = updated
        widened = updated.astype(jnp.float32)
        squares = widened * widened
        part = squares[:, :128]
        for c in range(1, width // 128):
            part += squares[:, c * 128:(c + 1) * 128]
        mine[b:b + 1, :] = jnp.sum(part.T, axis=0, keepdims=True)

    pl.semaphore_wait(barrier, size - 1)

    def copy(j):
        return pltpu.make_async_remote_copy(
            src_ref=mine, dst_ref=others.at[j], send_sem=send_sem.at[j], recv_sem=recv_sem.at[j],
            device_id={"tp": (me + j) % size}, device_id_type=pl.DeviceIdType.MESH)

    def send(j, _):
        copy(j).start()
        return 0

    lax.fori_loop(1, size, send, 0)

    def receive(j, total):
        copy(j).wait_recv()
        return total + others[j]

    total = lax.fori_loop(1, size, receive, mine[...])
    scale = lax.rsqrt(total / MODEL_WIDTH + 1e-05)
    gain = gain_ref[...].astype(jnp.float32)
    for b in range(blocks):
        rows = slice(b * 128, (b + 1) * 128)
        column = jnp.broadcast_to(scale[b:b + 1, :], (128, 128)).T
        for c in range(width // 128):
            cols = slice(c * 128, (c + 1) * 128)
            normed_ref[rows, cols] = (updated_ref[rows, cols].astype(jnp.float32) * column
                                      * gain[:, cols]).astype(jnp.bfloat16)

    def sent(j, _):
        copy(j).wait_send()
        return 0

    lax.fori_loop(1, size, sent, 0)


def expand_and_norm(size, rank, proj, residual, rank_rows, slot_rows, expand_flat, gain):
    count, width = residual.shape
    blocks = count // 128
    out = jax.ShapeDtypeStruct((count, width), jnp.bfloat16)
    return pl.pallas_call(
        functools.partial(norm_kernel, size, rank),
        out_shape=(out, out),
        in_specs=[pl.BlockSpec(memory_space=pltpu.VMEM)] * 6,
        out_specs=(pl.BlockSpec(memory_space=pltpu.VMEM),) * 2,
        scratch_shapes=[
            pltpu.VMEM((blocks, 128), jnp.float32),
            pltpu.VMEM((size, blocks, 128), jnp.float32),
            pltpu.SemaphoreType.DMA((size,)),
            pltpu.SemaphoreType.DMA((size,)),
        ],
        compiler_params=pltpu.CompilerParams(
            collective_id=1, has_side_effects=True, vmem_limit_bytes=48 * 1024 * 1024),
    )(proj, residual, rank_rows, slot_rows, expand_flat, gain)


def on_device(
    depth,
    pair,
    gate_up,
    residual,
    down_weight,
    shrink_weight,
    expand_weight,
    block_adapter,
    adapter_slot,
    norm_gain,
):
    count_of_rows, _, ff_local = gate_up.shape
    blocks = block_adapter.shape[0]
    adapters, _, rank = shrink_weight.shape
    column_count = expand_weight.shape[2]
    adapter_range = jnp.arange(adapters, dtype=jnp.int32)
    chosen = block_adapter[:, None] == adapter_range[None, :]
    slot_ids = jnp.sum(jnp.where(chosen, adapter_slot[None, :], 0), axis=1)
    slot_rows = jnp.broadcast_to(
        slot_ids[:, None, None], (blocks, count_of_rows // blocks, 128)).reshape(count_of_rows, 128)
    shrink_flat = shrink_weight.transpose(0, 2, 1).reshape(adapters * rank, ff_local)
    hidden, rank_terms = hidden_and_rank(gate_up, shrink_flat, slot_rows, rank)
    shrunk_rows = lax.psum(rank_terms, "tp")
    projection_sum = project(hidden, down_weight, depth, pair)
    return tuple(expand_and_norm(
        depth * pair, rank, projection_sum, residual, shrunk_rows, slot_rows,
        expand_weight.reshape(adapters * rank, column_count), norm_gain[None, :]))


def solution(mesh):
    in_specs = (
        P(("group", "dp"), None, "tp"),
        P(("group", "dp"), "tp"),
        P("tp", None),
        P(None, "tp", None),
        P(None, None, "tp"),
        P(("group", "dp")),
        P(),
        P("tp"),
    )
    out_specs = (P(("group", "dp"), "tp"), P(("group", "dp"), "tp"))
    pair = max(1, 4 // mesh.shape["group"])
    depth = mesh.shape["tp"] // pair
    return jax.shard_map(
        functools.partial(on_device, depth, pair),
        mesh=mesh, in_specs=in_specs, out_specs=out_specs, check_vma=False
    )
```

```python
import functools

import jax
import jax.numpy as jnp
from jax import lax
from jax.experimental import pallas as pl
from jax.experimental.pallas import tpu as pltpu
from jax.sharding import PartitionSpec as P

MODEL_WIDTH = 8192
CHUNK_ROWS = 128
COL_TILE = 256


adapter_scale = 0.5


def project_kernel(depth, pair, chunks, h_ref, w_hbm, out_ref, w_vmem, outgoing, held, landed, acc,
                   w_sem, pair_send, pair_recv, line_send, line_recv, *cross_refs):
    me = lax.axis_index("tp")
    pos = me // pair
    side = me % pair
    rows = CHUNK_ROWS
    width = acc.shape[1]
    tile = min(COL_TILE, width)
    first = 1 if cross_refs else 0
    toward = 2 * (pos // (depth // 2)) - 1

    def target(j):
        return (pos + toward * (1 + j) + depth) % depth

    def w_copy(block):
        return pltpu.make_async_copy(
            w_hbm.at[:, pl.ds(pl.multiple_of(block * width, width), width)],
            w_vmem.at[block], w_sem.at[block])

    def pair_copy(chunk, dest):
        return pltpu.make_async_remote_copy(
            src_ref=outgoing.at[chunk % 2, dest], dst_ref=held.at[chunk, dest],
            send_sem=pair_send.at[chunk, dest], recv_sem=pair_recv.at[chunk, dest],
            device_id={"tp": pos * pair + (1 - side)}, device_id_type=pl.DeviceIdType.MESH)

    def line_copy(chunk, dest, slot, to):
        return pltpu.make_async_remote_copy(
            src_ref=held.at[chunk, dest], dst_ref=landed.at[chunk, slot],
            send_sem=line_send.at[chunk, dest], recv_sem=line_recv.at[chunk, slot],
            device_id={"tp": to * pair + side}, device_id_type=pl.DeviceIdType.MESH)

    if cross_refs:
        cross_held, cross_landed, cross_send, cross_recv = cross_refs

        def cross_copy(dest, slot, to):
            return pltpu.make_async_remote_copy(
                src_ref=cross_held.at[dest], dst_ref=cross_landed.at[slot],
                send_sem=cross_send.at[dest], recv_sem=cross_recv.at[slot],
                device_id={"tp": to * pair + side}, device_id_type=pl.DeviceIdType.MESH)

        def swap_copy():
            return pltpu.make_async_remote_copy(
                src_ref=cross_held.at[pos], dst_ref=held.at[0, pos],
                send_sem=pair_send.at[0, pos], recv_sem=pair_recv.at[0, pos],
                device_id={"tp": pos * pair + (1 - side)}, device_id_type=pl.DeviceIdType.MESH)

    barrier = pltpu.get_barrier_semaphore()
    if pair > 1:
        pl.semaphore_signal(barrier, inc=1, device_id={"tp": pos * pair + (1 - side)},
                            device_id_type=pl.DeviceIdType.MESH)

    @pl.when(pos > 0)
    def _():
        pl.semaphore_signal(barrier, inc=1, device_id={"tp": me - pair},
                            device_id_type=pl.DeviceIdType.MESH)

    @pl.when(pos < depth - 1)
    def _():
        pl.semaphore_signal(barrier, inc=1, device_id={"tp": me + pair},
                            device_id_type=pl.DeviceIdType.MESH)

    def start_w(j, _):
        if pair > 1:
            w_copy(target(j) * pair + (1 - side)).start()
        return 0

    lax.fori_loop(0, depth, start_w, 0)

    def start_w_own(j, _):
        w_copy(target(j) * pair + side).start()
        return 0

    lax.fori_loop(0, depth, start_w_own, 0)

    pl.semaphore_wait(
        barrier, pair - 1 + jnp.minimum(pos, 1) + jnp.minimum(depth - 1 - pos, 1))

    def lines(chunk):
        return pl.ds(pl.multiple_of(chunk * rows, rows), rows)

    def offer(chunk):
        def one(j, _):
            dest = target(j)
            block = dest * pair + (1 - side)

            @pl.when(chunk == first)
            def _():
                w_copy(block).wait()

            @pl.when(chunk >= first + 2)
            def _():
                pair_copy(chunk - 2, dest).wait_send()

            def col(n, _):
                cols = pl.ds(pl.multiple_of(n * tile, tile), tile)
                outgoing[chunk % 2, dest, :, cols] = jnp.dot(
                    h_ref[lines(chunk), :], w_vmem[block, :, cols],
                    preferred_element_type=jnp.float32).astype(jnp.bfloat16)
                return 0

            lax.fori_loop(0, width // tile, col, 0)
            pair_copy(chunk, dest).start()
            return 0

        lax.fori_loop(0, depth, one, 0)

    def multiply(chunk, block):
        def col(n, _):
            cols = pl.ds(pl.multiple_of(n * tile, tile), tile)
            acc[:, cols] = jnp.dot(h_ref[lines(chunk), :], w_vmem[block, :, cols],
                                   preferred_element_type=jnp.float32)
            return 0

        lax.fori_loop(0, width // tile, col, 0)

    def gather_own(chunk, dest, opening):
        block = dest * pair + side

        @pl.when(chunk == opening)
        def _():
            w_copy(block).wait()

        multiply(chunk, block)
        if pair > 1:
            @pl.when(chunk >= first)
            def _():
                pair_copy(chunk, dest).wait_recv()
                acc[...] += held[chunk, dest].astype(jnp.float32)

    def take(chunk, slot):
        line_copy(chunk, 0, slot, pos).wait_recv()
        acc[...] += landed[chunk, slot].astype(jnp.float32)

    def cross_take(slot):
        cross_copy(0, slot, pos).wait_recv()
        acc[...] += cross_landed[slot].astype(jnp.float32)

    def below_slot(dest):
        return dest + (depth - dest) * (1 - jnp.minimum(pos - 1 - dest, 1))

    def forward(chunk, dest, up):
        gather_own(chunk, dest, 0)

        @pl.when(pos > 0 if up else pos < depth - 1)
        def _():
            take(chunk, dest)

        held[chunk, dest] = acc[...].astype(jnp.bfloat16)
        if up:
            line_copy(chunk, dest, dest, pos + 1).start()
        else:
            line_copy(chunk, dest, below_slot(dest), pos - 1).start()
        if cross_refs:
            @pl.when(chunk == 0)
            def _():
                multiply(0, dest * pair + (1 - side))

                @pl.when(pos > 0 if up else pos < depth - 1)
                def _():
                    cross_take(dest)

                cross_held[dest] = acc[...].astype(jnp.bfloat16)
                if up:
                    cross_copy(dest, dest, pos + 1).start()
                else:
                    cross_copy(dest, below_slot(dest), pos - 1).start()

    def send_up(chunk):
        def one(j, _):
            forward(chunk, depth - 1 - j, True)
            return 0

        lax.fori_loop(0, depth - 1 - pos, one, 0)

    def send_down(chunk):
        def one(j, _):
            forward(chunk, j, False)
            return 0

        lax.fori_loop(0, pos, one, 0)

    def keep(chunk):
        gather_own(chunk, pos, first)

        @pl.when(pos > 0)
        def _():
            take(chunk, pos)

        @pl.when(pos < depth - 1)
        def _():
            take(chunk, depth)

        if cross_refs:
            @pl.when(chunk == 0)
            def _():
                swap_copy().wait_recv()
                acc[...] += held[0, pos].astype(jnp.float32)

        out_ref[lines(chunk), :] = acc[...]

    def swap():
        multiply(0, pos * pair + (1 - side))

        @pl.when(pos > 0)
        def _():
            cross_take(pos)

        @pl.when(pos < depth - 1)
        def _():
            cross_take(depth)

        cross_held[pos] = acc[...].astype(jnp.bfloat16)
        swap_copy().start()

    def step(k, _):
        if pair > 1:
            @pl.when(k + first < chunks)
            def _():
                offer(k + first)

        upward = k + first - 1 - pos
        downward = k + first - depth + pos

        @pl.when(jnp.logical_and(upward >= 0, upward < chunks))
        def _():
            send_up(upward)

        @pl.when(jnp.logical_and(downward >= 0, downward < chunks))
        def _():
            send_down(downward)

        last = jnp.minimum(upward, downward)
        if cross_refs:
            @pl.when(last == 0)
            def _():
                swap()

        @pl.when(jnp.logical_and(last >= first, last < chunks))
        def _():
            keep(last)

        if cross_refs:
            @pl.when(last == first + 3)
            def _():
                keep(0)
        return 0

    lax.fori_loop(0, chunks + depth - first, step, 0)

    def finish(chunk, _):
        def one(dest, _):
            @pl.when(dest != pos)
            def _():
                line_copy(chunk, dest, dest, pos).wait_send()
            if pair > 1:
                @pl.when(chunk >= chunks - 2)
                def _():
                    pair_copy(chunk, dest).wait_send()
            if cross_refs:
                @pl.when(jnp.logical_and(chunk == 0, dest != pos))
                def _():
                    cross_copy(dest, dest, pos).wait_send()
            return 0

        lax.fori_loop(0, depth, one, 0)
        return 0

    lax.fori_loop(0, chunks, finish, 0)
    if cross_refs:
        swap_copy().wait_send()


def project(hidden, down_weight, depth, pair):
    count, inner = hidden.shape
    width = down_weight.shape[1] // (depth * pair)
    chunks = count // CHUNK_ROWS
    block = (CHUNK_ROWS, width)
    cross = [] if pair == 1 or chunks < 6 else [
        pltpu.VMEM((depth,) + block, jnp.bfloat16),
        pltpu.VMEM((depth + 1,) + block, jnp.bfloat16),
        pltpu.SemaphoreType.DMA((depth,)),
        pltpu.SemaphoreType.DMA((depth + 1,)),
    ]
    return pl.pallas_call(
        functools.partial(project_kernel, depth, pair, chunks),
        out_shape=jax.ShapeDtypeStruct((count, width), jnp.float32),
        in_specs=[pl.BlockSpec(memory_space=pltpu.VMEM), pl.BlockSpec(memory_space=pl.ANY)],
        out_specs=pl.BlockSpec(memory_space=pltpu.VMEM),
        scratch_shapes=[
            pltpu.VMEM((depth * pair, inner, width), jnp.bfloat16),
            pltpu.VMEM((2, depth if pair > 1 else 1) + block, jnp.bfloat16),
            pltpu.VMEM((chunks, depth) + block, jnp.bfloat16),
            pltpu.VMEM((chunks, depth + 1) + block, jnp.bfloat16),
            pltpu.VMEM(block, jnp.float32),
            pltpu.SemaphoreType.DMA((depth * pair,)),
            pltpu.SemaphoreType.DMA((chunks, depth)),
            pltpu.SemaphoreType.DMA((chunks, depth)),
            pltpu.SemaphoreType.DMA((chunks, depth)),
            pltpu.SemaphoreType.DMA((chunks, depth + 1)),
        ] + cross,
        compiler_params=pltpu.CompilerParams(
            collective_id=0, has_side_effects=True, vmem_limit_bytes=60 * 1024 * 1024),
        cost_estimate=pl.CostEstimate(
            flops=2 * count * inner * down_weight.shape[1],
            bytes_accessed=200_000_000, transcendentals=0),
    )(hidden, down_weight)


def slot_mask(slot_rows, group, rank):
    per = 128 // rank
    lane = lax.broadcasted_iota(jnp.int32, slot_rows.shape, 1) // rank
    return slot_rows == group * per + lane


def hidden_kernel(rank, gate_up_ref, shrink_ref, slot_ref, hidden_ref, rank_ref):
    gate = gate_up_ref[:, 0, :].astype(jnp.float32)
    up = gate_up_ref[:, 1, :].astype(jnp.float32)
    hidden = (jax.nn.silu(gate) * up).astype(jnp.bfloat16)
    hidden_ref[...] = hidden
    slot_rows = slot_ref[...]
    total = jnp.zeros(slot_rows.shape, jnp.float32)
    terms = lax.dot_general(hidden, shrink_ref[...], (((1,), (1,)), ((), ())),
                            preferred_element_type=jnp.float32)
    for group in range(shrink_ref.shape[0] // 128):
        part = terms[:, group * 128:(group + 1) * 128]
        total += jnp.where(slot_mask(slot_rows, group, rank), part, 0.0)
    rank_ref[...] = total.astype(jnp.bfloat16)


def hidden_and_rank(gate_up, shrink_flat, slot_rows, rank):
    count, _, inner = gate_up.shape
    rows = 128
    return pl.pallas_call(
        functools.partial(hidden_kernel, rank),
        grid=(count // rows,),
        out_shape=(jax.ShapeDtypeStruct((count, inner), jnp.bfloat16),
                   jax.ShapeDtypeStruct((count, 128), jnp.bfloat16)),
        in_specs=[pl.BlockSpec((rows, 2, inner), lambda i: (i, 0, 0)),
                  pl.BlockSpec(shrink_flat.shape, lambda i: (0, 0)),
                  pl.BlockSpec((rows, 128), lambda i: (i, 0))],
        out_specs=(pl.BlockSpec((rows, inner), lambda i: (i, 0)),
                   pl.BlockSpec((rows, 128), lambda i: (i, 0))),
        compiler_params=pltpu.CompilerParams(vmem_limit_bytes=48 * 1024 * 1024),
    )(gate_up, shrink_flat, slot_rows)


def norm_kernel(size, rank, proj_ref, residual_ref, rank_ref, slot_ref, expand_ref, gain_ref,
                updated_ref, normed_ref, mine, others, send_sem, recv_sem):
    me = lax.axis_index("tp")
    barrier = pltpu.get_barrier_semaphore()

    def greet(j, _):
        pl.semaphore_signal(barrier, inc=1, device_id={"tp": (me + j) % size},
                            device_id_type=pl.DeviceIdType.MESH)
        return 0

    lax.fori_loop(1, size, greet, 0)
    groups = expand_ref.shape[0] // 128
    width = updated_ref.shape[1]
    blocks = mine.shape[0]
    for b in range(blocks):
        rows = slice(b * 128, (b + 1) * 128)
        slot_rows = slot_ref[rows, :]
        values = rank_ref[rows, :].astype(jnp.float32)
        spread = jnp.concatenate(
            [jnp.where(slot_mask(slot_rows, group, rank), values, 0.0) for group in range(groups)],
            axis=1).astype(jnp.bfloat16)
        adapter_term = jnp.dot(spread, expand_ref[...], preferred_element_type=jnp.float32)
        updated = (residual_ref[rows, :].astype(jnp.float32) + proj_ref[rows, :]
                   + adapter_scale * adapter_term).astype(jnp.bfloat16)
        updated_ref[rows, :] = updated
        widened = updated.astype(jnp.float32)
        squares = widened * widened
        part = squares[:, :128]
        for c in range(1, width // 128):
            part += squares[:, c * 128:(c + 1) * 128]
        mine[b:b + 1, :] = jnp.sum(part.T, axis=0, keepdims=True)

    pl.semaphore_wait(barrier, size - 1)

    def copy(j):
        return pltpu.make_async_remote_copy(
            src_ref=mine, dst_ref=others.at[j], send_sem=send_sem.at[j], recv_sem=recv_sem.at[j],
            device_id={"tp": (me + j) % size}, device_id_type=pl.DeviceIdType.MESH)

    def send(j, _):
        copy(j).start()
        return 0

    lax.fori_loop(1, size, send, 0)

    def receive(j, total):
        copy(j).wait_recv()
        return total + others[j]

    total = lax.fori_loop(1, size, receive, mine[...])
    scale = lax.rsqrt(total / MODEL_WIDTH + 1e-05)
    gain = gain_ref[...].astype(jnp.float32)
    for b in range(blocks):
        rows = slice(b * 128, (b + 1) * 128)
        column = jnp.broadcast_to(scale[b:b + 1, :], (128, 128)).T
        for c in range(width // 128):
            cols = slice(c * 128, (c + 1) * 128)
            normed_ref[rows, cols] = (updated_ref[rows, cols].astype(jnp.float32) * column
                                      * gain[:, cols]).astype(jnp.bfloat16)

    def sent(j, _):
        copy(j).wait_send()
        return 0

    lax.fori_loop(1, size, sent, 0)


def expand_and_norm(size, rank, proj, residual, rank_rows, slot_rows, expand_flat, gain):
    count, width = residual.shape
    blocks = count // 128
    out = jax.ShapeDtypeStruct((count, width), jnp.bfloat16)
    return pl.pallas_call(
        functools.partial(norm_kernel, size, rank),
        out_shape=(out, out),
        in_specs=[pl.BlockSpec(memory_space=pltpu.VMEM)] * 6,
        out_specs=(pl.BlockSpec(memory_space=pltpu.VMEM),) * 2,
        scratch_shapes=[
            pltpu.VMEM((blocks, 128), jnp.float32),
            pltpu.VMEM((size, blocks, 128), jnp.float32),
            pltpu.SemaphoreType.DMA((size,)),
            pltpu.SemaphoreType.DMA((size,)),
        ],
        compiler_params=pltpu.CompilerParams(
            collective_id=1, has_side_effects=True, vmem_limit_bytes=48 * 1024 * 1024),
    )(proj, residual, rank_rows, slot_rows, expand_flat, gain)


def on_device(
    depth,
    pair,
    gate_up,
    residual,
    down_weight,
    shrink_weight,
    expand_weight,
    block_adapter,
    adapter_slot,
    norm_gain,
):
    count_of_rows, _, ff_local = gate_up.shape
    blocks = block_adapter.shape[0]
    adapters, _, rank = shrink_weight.shape
    column_count = expand_weight.shape[2]
    adapter_range = jnp.arange(adapters, dtype=jnp.int32)
    chosen = block_adapter[:, None] == adapter_range[None, :]
    slot_ids = jnp.sum(jnp.where(chosen, adapter_slot[None, :], 0), axis=1)
    slot_rows = jnp.broadcast_to(
        slot_ids[:, None, None], (blocks, count_of_rows // blocks, 128)).reshape(count_of_rows, 128)
    shrink_flat = shrink_weight.transpose(0, 2, 1).reshape(adapters * rank, ff_local)
    hidden, rank_terms = hidden_and_rank(gate_up, shrink_flat, slot_rows, rank)
    shrunk_rows = lax.psum(rank_terms, "tp")
    projection_sum = project(hidden, down_weight, depth, pair)
    return tuple(expand_and_norm(
        depth * pair, rank, projection_sum, residual, shrunk_rows, slot_rows,
        expand_weight.reshape(adapters * rank, column_count), norm_gain[None, :]))


def solution(mesh):
    in_specs = (
        P(("group", "dp"), None, "tp"),
        P(("group", "dp"), "tp"),
        P("tp", None),
        P(None, "tp", None),
        P(None, None, "tp"),
        P(("group", "dp")),
        P(),
        P("tp"),
    )
    out_specs = (P(("group", "dp"), "tp"), P(("group", "dp"), "tp"))
    pair = max(1, 4 // mesh.shape["group"])
    depth = mesh.shape["tp"] // pair
    return jax.shard_map(
        functools.partial(on_device, depth, pair),
        mesh=mesh, in_specs=in_specs, out_specs=out_specs, check_vma=False
    )
```
